32 devices in a mesh: groups: 2 (over x), col: 4 (over y, core), load: 4 (over z).
Axes of the slice: x: 2, y: 2, z: 4, core: 2. Of those that a mesh axis runs over, the one named last changes fastest.
Arguments:
- load_cols: bfloat16 [4, 4, 640, 8192], P(None, 'col', None, ('groups', 'load')), parts along dimension 3, may hold values from -40 to 40
- weights: float32 [8192], P(('groups', 'load')), parts along dimension 0, may hold values from 0.5 to 12
- inv_diag: bfloat16 [4, 4, 640, 640], P(None, 'col'), may hold values from -1.5 to 1.5, as said below
- off_diag: bfloat16 [3, 4, 640, 640], P(None, 'col'), may hold values from -0.125 to 0.125
- crosses: int32 [3, 4], P(None, 'col'), may hold values 0 or 1
- members: int32 [4, 4, 4, 2], P(None, 'col'), may hold values from 0 to 4
- stiffness: bfloat16 [4, 4, 4, 256, 256], P(None, 'col'), may hold values from -2 to 2
Outputs:
- solution: bfloat16 [4, 4, 640, 8192], P(None, 'col', None, ('groups', 'load')), parts along dimension 3
- sensitivity: float32 [8, 4, 4], P('groups', 'col'), parts along dimension 0
The draws below stay inside these ranges and needn't reach their ends.
There are 2 independent parts, one for each index of `groups`. The reference program is written for one: setup_inputs(seed, part) draws one part's arguments, and reference() takes and returns one part's arrays. A program takes and returns all parts, laid end to end along the dimension named above; an argument that names none is the same for every part. Nothing has to cross between parts.
Inputs may be any that keep to these rules, and one draw needn't show every extreme that they name: `inv_diag`: each block is lower triangular with its diagonal between 0.7 and 1.4.
All inputs are finite; a program needn't handle non-finite values. No bound on the sum of `crosses` on one device may be relied on, other than what follows from the above.
Results may differ from the reference program's by a relative error of at most 0.007.
Values may be sent and summed in bfloat16 or wider, within the bound.
A program may use at most 128 MiB of HBM per device.

```python
import jax
import jax.numpy as jnp

BLK = 128
SB = 5
S = 640
LEV = 4
GRP = 4
NRHS = 4096
NSN = 4
N_COL = 4


def draw_load_cols(key, part):
    key = jax.random.fold_in(key, 11)
    keys = jax.random.split(key, 5)
    shape = (LEV, NSN, S, NRHS)
    row_scale = jnp.exp(jax.random.uniform(keys[0], (LEV, NSN, S, 1), jnp.float32, -1.15, 1.15))
    col_scale = jnp.exp(jax.random.uniform(keys[1], (1, 1, 1, NRHS), jnp.float32, -1.15, 1.15))
    rough = jnp.clip(jax.random.normal(keys[2], shape, jnp.float32), -3.5, 3.5)
    col_common = jnp.clip(jax.random.normal(keys[4], (LEV, NSN, 1, NRHS), jnp.float32), -2.2, 2.2)
    base = 0.6 * rough + 0.8 * col_common
    return (row_scale * col_scale * base).astype(jnp.bfloat16)


def draw_weights(key, part):
    key = jax.random.fold_in(key, 12)
    position = jnp.arange(NRHS, dtype=jnp.float32) / NRHS
    factor = jnp.exp(jax.random.uniform(key, (NRHS,), jnp.float32, -0.35, 0.35))
    return (jnp.exp(position * jnp.log(3.0)) * factor).astype(jnp.float32)


def draw_inv_diag(key, part):
    key = jax.random.fold_in(key, 13)
    keys = jax.random.split(key, 2)
    shape = (LEV, NSN, S, S)
    rows = jax.lax.broadcasted_iota(jnp.int32, shape, 2)
    cols = jax.lax.broadcasted_iota(jnp.int32, shape, 3)
    diag_part = jnp.exp(jax.random.uniform(keys[0], shape, jnp.float32, jnp.log(0.7), jnp.log(1.4)))
    lower = jnp.clip(jax.random.normal(keys[1], shape, jnp.float32), -6.0, 6.0)
    lower = lower * (0.5 / jnp.sqrt(float(S)))
    values = jnp.where(rows == cols, diag_part, jnp.where(cols < rows, lower, 0.0))
    return values.astype(jnp.bfloat16)


def draw_stiffness(key, part):
    key = jax.random.fold_in(key, 14)
    keys = jax.random.split(key, 2)
    shape = (LEV, NSN, GRP, 2 * BLK, 2 * BLK)
    rows = jax.lax.broadcasted_iota(jnp.int32, shape, 3)
    cols = jax.lax.broadcasted_iota(jnp.int32, shape, 4)
    diag_part = jnp.exp(jax.random.uniform(keys[0], shape, jnp.float32, jnp.log(0.5), jnp.log(2.0)))
    coupling = jnp.clip(jax.random.normal(keys[1], shape, jnp.float32), -6.0, 6.0)
    coupling = coupling * (1.5 / jnp.sqrt(float(2 * BLK)))
    return jnp.where(rows == cols, diag_part, coupling).astype(jnp.bfloat16)


def with_ends(drawn, key, smallest, high):
    longest = drawn.shape.index(max(drawn.shape))
    spots = []
    for shift in (0, 1):
        where = [jax.random.randint(jax.random.fold_in(key, axis), (), 0, length) for axis, length in enumerate(drawn.shape)]
        where[longest] = (where[longest] + shift) % drawn.shape[longest]
        spots.append(tuple(where))
    return drawn.at[spots[0]].set(smallest).at[spots[1]].set(high)


def steps_of(own_key, extent, shards, smallest, high):
    gain = 1.0
    for axis_at, blocks in shards:
        heights = jax.random.uniform(jax.random.fold_in(jax.random.fold_in(own_key, 6), axis_at), (blocks,), jnp.float32, smallest / len(shards), high / len(shards))
        gain = gain * jnp.repeat(jnp.exp(heights), extent[axis_at] // blocks).reshape((-1,) + (1,) * (len(extent) - 1 - axis_at))
    return gain


def gaussian(stream_key, extent, deviation, bound, shards=(), held_as=jnp.bfloat16):
    drawn = jax.random.normal(stream_key, extent, jnp.float32) * deviation
    if len(shards) > 0:
        drawn = steps_of(stream_key, extent, shards, -0.22, 0.18) * drawn
    return jnp.clip(drawn, min=-bound, max=bound).astype(held_as)


def setup_inputs(seed: int = 0, part: int = 0) -> dict:
    key_list = jax.random.split(jax.random.key(seed), 8)
    part_keys = jax.random.split(jax.random.fold_in(key_list[7], part), 8)
    return {
        "load_cols": draw_load_cols(jax.random.fold_in(jax.random.fold_in(key_list[7], part), 71), part),
        "weights": draw_weights(jax.random.fold_in(jax.random.fold_in(key_list[7], part), 71), part),
        "inv_diag": draw_inv_diag(jax.random.fold_in(key_list[7], 71), part),
        "off_diag": gaussian(key_list[3], (LEV - 1, NSN, S, S), (4 * S) ** -0.5, 0.125, ((1, 4),)),
        "crosses": with_ends((jax.random.randint(key_list[4], (LEV - 1, NSN), 0, 2) < 1).astype(jnp.int32), jax.random.fold_in(key_list[4], 1), 0, 1),
        "members": with_ends(jax.random.randint(key_list[5], (LEV, NSN, GRP, 2), 0, SB), jax.random.fold_in(key_list[5], 1), 0, SB - 1).astype(jnp.int32),
        "stiffness": draw_stiffness(jax.random.fold_in(key_list[7], 71), part),
    }


def apply_blocks(matrices, columns):
    return jnp.einsum("nij,njk->nik", matrices.astype(jnp.float32), columns.astype(jnp.float32))


def apply_transposed(matrices, columns):
    return jnp.einsum("nji,njk->nik", matrices.astype(jnp.float32), columns.astype(jnp.float32))


def reference(load_cols, weights, inv_diag, off_diag, crosses, members, stiffness):
    bit_count = N_COL.bit_length() - 1
    node_index = jnp.arange(NSN, dtype=jnp.int32)
    incoming = jnp.zeros((NSN, S, NRHS), jnp.float32)
    forward_parts = []
    for level_index in range(LEV):
        right_side = (load_cols[level_index].astype(jnp.float32) - incoming).astype(jnp.bfloat16)
        forward_now = apply_blocks(inv_diag[level_index], right_side).astype(jnp.bfloat16)
        forward_parts.append(forward_now)
        if level_index + 1 < LEV:
            update = apply_blocks(off_diag[level_index], forward_now).astype(jnp.bfloat16)
            crossing = (crosses[level_index] == 1)[:, None, None]
            outgoing = jnp.where(crossing, update, jnp.zeros_like(update))
            retained = jnp.where(crossing, jnp.zeros_like(update), update)
            partner = jnp.bitwise_xor(node_index, 1 << (level_index % bit_count))
            incoming = retained.astype(jnp.float32) + outgoing[partner].astype(jnp.float32)
    results = [None] * LEV
    sens_parts = [None] * LEV
    upper_part = None
    for level_index in reversed(range(LEV)):
        if level_index + 1 < LEV:
            crossing = (crosses[level_index] == 1)[:, None, None]
            partner = jnp.bitwise_xor(node_index, 1 << (level_index % bit_count))
            parent_cols = jnp.where(crossing, upper_part[partner], upper_part)
            pulled = apply_transposed(off_diag[level_index], parent_cols)
            target = (forward_parts[level_index].astype(jnp.float32) - pulled).astype(jnp.bfloat16)
        else:
            target = forward_parts[level_index]
        answer = apply_transposed(inv_diag[level_index], target).astype(jnp.bfloat16)
        results[level_index] = answer
        upper_part = answer
        blocks = answer.astype(jnp.float32).reshape(NSN, SB, BLK, NRHS)
        onehot = (members[level_index][..., None] == jnp.arange(SB, dtype=jnp.int32)).astype(jnp.float32)
        picked = jnp.einsum("ngas,nsbk->ngabk", onehot, blocks).reshape(NSN, GRP, 2 * BLK, NRHS)
        pushed = jnp.einsum("ngij,ngjk->ngik", stiffness[level_index].astype(jnp.float32), picked)
        sens_parts[level_index] = jnp.sum(picked * pushed * weights, axis=(2, 3)) / (NRHS * 2 * BLK)
    return jnp.stack(results), jnp.stack(sens_parts)
```

```python
import functools

import jax
import jax.numpy as jnp
from jax import lax
from jax.experimental import pallas as pl
from jax.experimental.pallas import tpu as pltpu
from jax.sharding import PartitionSpec as P

MESH = pl.DeviceIdType.MESH
TILE = 256
PART = 256
BLK = 128


def row_tiles(size):
    return [(start, min(start + TILE, size)) for start in range(0, size, TILE)]


def lower_rows(matrix, columns):
    for start, end in row_tiles(matrix.shape[0]):
        yield start, end, jnp.dot(
            matrix[start:end, :end], columns[:end, :], preferred_element_type=jnp.float32
        )


def upper_rows(matrix, columns):
    for start, end in row_tiles(matrix.shape[0]):
        yield start, end, jnp.dot(
            matrix[start:end, start:], columns[start:, :], preferred_element_type=jnp.float32
        )


def full_rows(matrix, columns):
    for start, end in row_tiles(matrix.shape[0]):
        yield start, end, jnp.dot(
            matrix[start:end, :], columns[...], preferred_element_type=jnp.float32
        )


def kernel(
    col_count,
    load_count,
    load_hbm,
    weights,
    inv_hbm,
    off_hbm,
    crosses,
    members,
    stiff_hbm,
    out_hbm,
    energy_out,
    work,
    solved,
    kept,
    outgoing,
    up_land,
    down_land,
    rhs,
    inv,
    off,
    inv_t,
    off_t,
    stiff,
    energy,
    energy_sum,
    energy_land,
    load_sem,
    inv_sem,
    off_sem,
    stiff_sem,
    out_sem,
    up_send,
    up_recv,
    down_send,
    down_recv,
    energy_send,
    energy_recv,
):
    levels, parts, rows, part_cols = work.shape
    groups = stiff.shape[1]
    bit_count = col_count.bit_length() - 1
    my_col = lax.axis_index("col")
    my_load = lax.axis_index("load")

    def partner(level):
        mask = 1 << (level % bit_count)
        return my_col + mask - 2 * mask * (my_col // mask % 2)

    def load_peer(step):
        return lax.rem(my_load + step, load_count)

    def load_copy(level, part):
        start = part * part_cols
        return pltpu.make_async_copy(
            load_hbm.at[level, 0, :, pl.ds(pl.multiple_of(start, part_cols), part_cols)],
            work.at[level, part],
            load_sem.at[level, part],
        )

    def inv_copy(level):
        return pltpu.make_async_copy(inv_hbm.at[level, 0], inv.at[level], inv_sem.at[level])

    def off_copy(level):
        return pltpu.make_async_copy(off_hbm.at[level, 0], off.at[level], off_sem.at[level])

    def stiff_copy(level):
        return pltpu.make_async_copy(stiff_hbm.at[level, 0], stiff.at[level], stiff_sem.at[level])

    def out_copy(level, part):
        start = part * part_cols
        return pltpu.make_async_copy(
            solved.at[level, part],
            out_hbm.at[level, 0, :, pl.ds(pl.multiple_of(start, part_cols), part_cols)],
            out_sem.at[level, part],
        )

    def up_copy(level, part):
        return pltpu.make_async_remote_copy(
            src_ref=outgoing.at[level, part],
            dst_ref=up_land.at[level, part],
            send_sem=up_send.at[level, part],
            recv_sem=up_recv.at[level, part],
            device_id={"col": partner(level)},
            device_id_type=MESH,
        )

    def down_copy(level, part):
        return pltpu.make_async_remote_copy(
            src_ref=solved.at[level + 1, part],
            dst_ref=down_land.at[level, part],
            send_sem=down_send.at[level, part],
            recv_sem=down_recv.at[level, part],
            device_id={"col": partner(level)},
            device_id_type=MESH,
        )

    def energy_copy(step):
        return pltpu.make_async_remote_copy(
            src_ref=energy_sum,
            dst_ref=energy_land.at[step - 1],
            send_sem=energy_send.at[step - 1],
            recv_sem=energy_recv.at[step - 1],
            device_id={"load": load_peer(step)},
            device_id_type=MESH,
        )

    barrier = pltpu.get_barrier_semaphore()
    used_bits = sorted({level % bit_count for level in range(levels - 1)})
    for bit in used_bits:
        pl.semaphore_signal(
            barrier, inc=1, device_id={"col": partner(bit)}, device_id_type=MESH
        )
    for step in range(1, load_count):
        pl.semaphore_signal(
            barrier, inc=1, device_id={"load": load_peer(step)}, device_id_type=MESH
        )

    inv_copy(0).start()
    load_copy(0, 0).start()
    off_copy(0).start()
    inv_copy(1).start()
    load_copy(0, 1).start()
    load_copy(1, 0).start()
    off_copy(1).start()
    load_copy(1, 1).start()
    for part in range(2, parts):
        load_copy(0, part).start()
        load_copy(1, part).start()
    for level in range(2, levels):
        inv_copy(level).start()
        if level + 1 < levels:
            off_copy(level).start()
        for part in range(parts):
            load_copy(level, part).start()
    for level in reversed(range(levels)):
        stiff_copy(level).start()

    energy[...] = jnp.zeros_like(energy)

    def crosses_here(level, shape):
        return jnp.full(shape, crosses[level, 0], jnp.int32) == 1

    def go_up(level, part):
        load_copy(level, part).wait()
        if level == 0:
            right_side = work.at[level, part]
        else:
            up_copy(level - 1, part).wait_recv()
            incoming = kept[level - 1, part].astype(jnp.float32) + up_land[
                level - 1, part
            ].astype(jnp.float32)
            rhs[...] = (work[level, part].astype(jnp.float32) - incoming).astype(jnp.bfloat16)
            right_side = rhs
        results = [
            (start, end, value.astype(jnp.bfloat16))
            for start, end, value in lower_rows(inv.at[level], right_side)
        ]
        for start, end, value in results:
            work[level, part, start:end, :] = value
        if level + 1 < levels:
            for start, end, value in full_rows(off.at[level], work.at[level, part]):
                crossing = crosses_here(level, value.shape)
                outgoing[level, part, start:end, :] = jnp.where(crossing, value, 0.0).astype(
                    jnp.bfloat16
                )
                kept[level, part, start:end, :] = jnp.where(crossing, 0.0, value).astype(
                    jnp.bfloat16
                )
            up_copy(level, part).start()

    def go_down(level, part):
        if level + 1 < levels:
            down_copy(level, part).wait_recv()
            rhs[...] = jnp.where(
                crosses_here(level, rhs.shape),
                down_land[level, part].astype(jnp.float32),
                solved[level + 1, part].astype(jnp.float32),
            ).astype(jnp.bfloat16)
            for start, end, value in full_rows(off_t.at[level], rhs):
                forward = work[level, part, start:end, :].astype(jnp.float32)
                work[level, part, start:end, :] = (forward - value).astype(jnp.bfloat16)
        for start, end, value in upper_rows(inv_t.at[level], work.at[level, part]):
            solved[level, part, start:end, :] = value.astype(jnp.bfloat16)
        if level > 0:
            down_copy(level - 1, part).start()
        out_copy(level, part).start()

    def picked(level, part, member):
        wanted = jnp.full((BLK, part_cols), member, jnp.int32)
        value = solved[level, part, :BLK, :].astype(jnp.float32)
        for block in range(1, rows // BLK):
            other = solved[level, part, block * BLK : (block + 1) * BLK, :]
            value = jnp.where(wanted == block, other.astype(jnp.float32), value)
        return value

    def add_energy(level, part):
        start = pl.multiple_of(part * part_cols, part_cols)
        spectral = weights[:, pl.ds(start, part_cols)]
        for group in range(groups):
            halves = [picked(level, part, members[level, 0, group, half]) for half in (0, 1)]
            stacked = jnp.concatenate(halves, axis=0)
            pushed = jnp.dot(
                stiff[level, group],
                stacked.astype(jnp.bfloat16),
                preferred_element_type=jnp.float32,
            )
            product = stacked * pushed
            folded = jnp.sum(product.reshape(-1, 8, part_cols), axis=0)
            energy[level * groups + group] += folded * spectral

    def turn(source, target):
        for start in range(0, rows, BLK):
            target[:, start : start + BLK] = source[start : start + BLK, :].T

    inv_copy(0).wait()
    off_copy(0).wait()

    def first(step, carry):
        @pl.when(step < parts)
        def _():
            go_up(0, step)

        @pl.when(step == 0)
        def _():
            inv_copy(1).wait()
            off_copy(1).wait()

        @pl.when(step > 0)
        def _():
            go_up(1, step - 1)

        return carry

    pl.semaphore_wait(barrier, len(used_bits) + load_count - 1)
    lax.fori_loop(0, parts + 1, first, 0)

    for level in range(2, levels):
        inv_copy(level).wait()
        if level + 1 < levels:
            off_copy(level).wait()
    for level in reversed(range(levels)):
        turn(inv.at[level], inv_t.at[level])
        if level + 1 < levels:
            turn(off.at[level], off_t.at[level])
    for level in range(levels):
        stiff_copy(level).wait()

    def second(step, carry):
        @pl.when(step >= 2)
        def _():
            go_down(2, step - 2)

        @pl.when((step >= 1) & (step < parts + 1))
        def _():
            go_up(3, step - 1)
            go_down(3, step - 1)

        @pl.when(step >= 2)
        def _():
            add_energy(3, step - 2)
            add_energy(2, step - 2)

        @pl.when(step < parts)
        def _():
            go_up(2, step)

        return carry

    lax.fori_loop(0, parts + 2, second, 0)

    def third(step, carry):
        @pl.when(step < parts)
        def _():
            go_down(1, step)
            add_energy(1, step)

        @pl.when(step > 0)
        def _():
            go_down(0, step - 1)
            add_energy(0, step - 1)

        return carry

    lax.fori_loop(0, parts + 1, third, 0)

    by_lane = jnp.sum(energy[...], axis=1)
    folded = by_lane[:, :128]
    for start in range(128, part_cols, 128):
        folded = folded + by_lane[:, start : start + 128]
    energy_sum[...] = folded
    for step in range(1, load_count):
        energy_copy(step).start()
    total = folded
    for step in range(1, load_count):
        energy_copy(step).wait_recv()
        total = total + energy_land[step - 1]
    totals = jnp.sum(total, axis=1, keepdims=True) * (
        1.0 / (load_count * parts * part_cols * stiff.shape[2])
    )
    shape = (levels * groups, 128)
    lane = lax.broadcasted_iota(jnp.int32, shape, 1)
    row = lax.broadcasted_iota(jnp.int32, shape, 0)
    spread = jnp.where(lane == row % groups, jnp.broadcast_to(totals, shape), 0.0)
    for level in range(levels):
        energy_out[level : level + 1, :] = jnp.sum(
            spread[level * groups : (level + 1) * groups], axis=0, keepdims=True
        )[:, :groups]

    def finish(part, carry):
        for level in range(levels):
            out_copy(level, part).wait()
        for level in range(levels - 1):
            up_copy(level, part).wait_send()
            down_copy(level, part).wait_send()
        return carry

    lax.fori_loop(0, parts, finish, 0)
    for step in range(1, load_count):
        energy_copy(step).wait_send()


def on_device(col_count, load_count, *args):
    load_cols, weights, inv_diag, off_diag, crosses, members, stiffness = args
    levels, _, rows, local_cols = load_cols.shape
    groups, pair_rows = stiffness.shape[2:4]
    part_cols = PART if local_cols % PART == 0 else local_cols
    parts = local_cols // part_cols
    dense = jnp.bfloat16
    buffer = (parts, rows, part_cols)
    dma = pltpu.SemaphoreType.DMA
    anywhere = pl.BlockSpec(memory_space=pl.ANY)
    in_vmem = pl.BlockSpec(memory_space=pltpu.VMEM)
    in_smem = pl.BlockSpec(memory_space=pltpu.SMEM)
    solved, energy = pl.pallas_call(
        functools.partial(kernel, col_count, load_count),
        out_shape=(
            jax.ShapeDtypeStruct(load_cols.shape, dense),
            jax.ShapeDtypeStruct((levels, groups), jnp.float32),
        ),
        in_specs=[anywhere, in_vmem, anywhere, anywhere, in_smem, in_smem, anywhere],
        out_specs=(anywhere, in_vmem),
        scratch_shapes=[
            pltpu.VMEM((levels,) + buffer, dense),
            pltpu.VMEM((levels,) + buffer, dense),
            pltpu.VMEM((levels - 1,) + buffer, dense),
            pltpu.VMEM((levels - 1,) + buffer, dense),
            pltpu.VMEM((levels - 1,) + buffer, dense),
            pltpu.VMEM((levels - 1,) + buffer, dense),
            pltpu.VMEM((rows, part_cols), dense),
            pltpu.VMEM((levels, rows, rows), dense),
            pltpu.VMEM((levels - 1, rows, rows), dense),
            pltpu.VMEM((levels, rows, rows), dense),
            pltpu.VMEM((levels - 1, rows, rows), dense),
            pltpu.VMEM((levels, groups, pair_rows, pair_rows), dense),
            pltpu.VMEM((levels * groups, 8, part_cols), jnp.float32),
            pltpu.VMEM((levels * groups, 128), jnp.float32),
            pltpu.VMEM((load_count - 1, levels * groups, 128), jnp.float32),
            dma((levels, parts)),
            dma((levels,)),
            dma((levels - 1,)),
            dma((levels,)),
            dma((levels, parts)),
            dma((levels - 1, parts)),
            dma((levels - 1, parts)),
            dma((levels - 1, parts)),
            dma((levels - 1, parts)),
            dma((load_count - 1,)),
            dma((load_count - 1,)),
        ],
        compiler_params=pltpu.CompilerParams(
            collective_id=0, has_side_effects=True, vmem_limit_bytes=56 * 2**20
        ),
    )(
        load_cols,
        weights.reshape(1, local_cols),
        inv_diag,
        off_diag,
        crosses,
        members,
        stiffness,
    )
    return solved, energy.reshape(levels, 1, groups)


def solution(mesh):
    placed = (
        P(None, "col", None, ("groups", "load")),
        P(("groups", "load")),
        P(None, "col", None, None),
        P(None, "col", None, None),
        P(None, "col"),
        P(None, "col", None, None),
        P(None, "col", None, None, None),
    )
    return jax.shard_map(
        functools.partial(on_device, mesh.shape["col"], mesh.shape["load"]),
        mesh=mesh,
        in_specs=placed,
        out_specs=(P(None, "col", None, ("groups", "load")), P("groups", "col", None)),
        check_vma=False,
    )
```

```python
import functools

import jax
import jax.numpy as jnp
from jax import lax
from jax.experimental import pallas as pl
from jax.experimental.pallas import tpu as pltpu
from jax.sharding import PartitionSpec as P

MESH = pl.DeviceIdType.MESH
TILE = 256
PART = 256
BLK = 128


def row_tiles(size):
    return [(start, min(start + TILE, size)) for start in range(0, size, TILE)]


def lower_rows(matrix, columns):
    for start, end in row_tiles(matrix.shape[0]):
        yield start, end, jnp.dot(
            matrix[start:end, :end], columns[:end, :], preferred_element_type=jnp.float32
        )


def upper_rows(matrix, columns):
    for start, end in row_tiles(matrix.shape[0]):
        yield start, end, jnp.dot(
            matrix[start:end, start:], columns[start:, :], preferred_element_type=jnp.float32
        )


def full_rows(matrix, columns):
    for start, end in row_tiles(matrix.shape[0]):
        yield start, end, jnp.dot(
            matrix[start:end, :], columns[...], preferred_element_type=jnp.float32
        )


def kernel(
    col_count,
    load_count,
    load_hbm,
    weights,
    inv_hbm,
    off_hbm,
    packed,
    stiff_hbm,
    out_hbm,
    energy_out,
    work,
    solved,
    kept,
    outgoing,
    up_land,
    down_land,
    rhs,
    inv,
    off,
    inv_t,
    off_t,
    stiff,
    energy,
    energy_sum,
    energy_land,
    load_sem,
    inv_sem,
    off_sem,
    stiff_sem,
    out_sem,
    up_send,
    up_recv,
    down_send,
    down_recv,
    energy_send,
    energy_recv,
):
    levels, parts, rows, part_cols = work.shape
    groups = stiff.shape[1]
    bit_count = col_count.bit_length() - 1
    my_col = lax.axis_index("col")
    my_load = lax.axis_index("load")

    def partner(level):
        mask = 1 << (level % bit_count)
        return my_col + mask - 2 * mask * (my_col // mask % 2)

    def load_peer(step):
        return lax.rem(my_load + step, load_count)

    def load_copy(level, part):
        start = part * part_cols
        return pltpu.make_async_copy(
            load_hbm.at[level, 0, :, pl.ds(pl.multiple_of(start, part_cols), part_cols)],
            work.at[level, part],
            load_sem.at[level, part],
        )

    def inv_copy(level):
        return pltpu.make_async_copy(inv_hbm.at[level, 0], inv.at[level], inv_sem.at[level])

    def off_copy(level):
        return pltpu.make_async_copy(off_hbm.at[level, 0], off.at[level], off_sem.at[level])

    def stiff_copy(level):
        return pltpu.make_async_copy(stiff_hbm.at[level, 0], stiff.at[level], stiff_sem.at[level])

    def out_copy(level, part):
        start = part * part_cols
        return pltpu.make_async_copy(
            solved.at[level, part],
            out_hbm.at[level, 0, :, pl.ds(pl.multiple_of(start, part_cols), part_cols)],
            out_sem.at[level, part],
        )

    def up_copy(level, part):
        return pltpu.make_async_remote_copy(
            src_ref=outgoing.at[level, part],
            dst_ref=up_land.at[level, part],
            send_sem=up_send.at[level, part],
            recv_sem=up_recv.at[level, part],
            device_id={"col": partner(level)},
            device_id_type=MESH,
        )

    def down_copy(level, part):
        return pltpu.make_async_remote_copy(
            src_ref=solved.at[level + 1, part],
            dst_ref=down_land.at[level, part],
            send_sem=down_send.at[level, part],
            recv_sem=down_recv.at[level, part],
            device_id={"col": partner(level)},
            device_id_type=MESH,
        )

    def energy_copy(step):
        return pltpu.make_async_remote_copy(
            src_ref=energy_sum,
            dst_ref=energy_land.at[step - 1],
            send_sem=energy_send.at[step - 1],
            recv_sem=energy_recv.at[step - 1],
            device_id={"load": load_peer(step)},
            device_id_type=MESH,
        )

    barrier = pltpu.get_barrier_semaphore()
    used_bits = sorted({level % bit_count for level in range(levels - 1)})
    for bit in used_bits:
        pl.semaphore_signal(
            barrier, inc=1, device_id={"col": partner(bit)}, device_id_type=MESH
        )
    for step in range(1, load_count):
        pl.semaphore_signal(
            barrier, inc=1, device_id={"load": load_peer(step)}, device_id_type=MESH
        )

    inv_copy(0).start()
    load_copy(0, 0).start()
    off_copy(0).start()
    inv_copy(1).start()
    load_copy(0, 1).start()
    load_copy(1, 0).start()
    off_copy(1).start()
    load_copy(1, 1).start()
    for part in range(2, parts):
        load_copy(0, part).start()
        load_copy(1, part).start()
    for level in range(2, levels):
        inv_copy(level).start()
        if level + 1 < levels:
            off_copy(level).start()
        for part in range(parts):
            load_copy(level, part).start()
    for level in reversed(range(levels)):
        stiff_copy(level).start()

    energy[...] = jnp.zeros_like(energy)

    def greeted():
        pl.semaphore_wait(barrier, len(used_bits) + load_count - 1)

    def crosses_here(level, shape):
        return jnp.full(shape, packed[level], jnp.int32) == 1

    def go_up(level, part):
        load_copy(level, part).wait()
        if level == 0:
            right_side = work.at[level, part]
        else:
            up_copy(level - 1, part).wait_recv()
            incoming = kept[level - 1, part].astype(jnp.float32) + up_land[
                level - 1, part
            ].astype(jnp.float32)
            rhs[...] = (work[level, part].astype(jnp.float32) - incoming).astype(jnp.bfloat16)
            right_side = rhs
        results = [
            (start, end, value.astype(jnp.bfloat16))
            for start, end, value in lower_rows(inv.at[level], right_side)
        ]
        for start, end, value in results:
            work[level, part, start:end, :] = value
        if level + 1 < levels:
            for start, end, value in full_rows(off.at[level], work.at[level, part]):
                crossing = crosses_here(level, value.shape)
                outgoing[level, part, start:end, :] = jnp.where(crossing, value, 0.0).astype(
                    jnp.bfloat16
                )
                kept[level, part, start:end, :] = jnp.where(crossing, 0.0, value).astype(
                    jnp.bfloat16
                )
            if level == 0:
                pl.when(part == 0)(greeted)
            up_copy(level, part).start()

    def go_down(level, part):
        if level + 1 < levels:
            down_copy(level, part).wait_recv()
            rhs[...] = jnp.where(
                crosses_here(level, rhs.shape),
                down_land[level, part].astype(jnp.float32),
                solved[level + 1, part].astype(jnp.float32),
            ).astype(jnp.bfloat16)
            for start, end, value in full_rows(off_t.at[level], rhs):
                forward = work[level, part, start:end, :].astype(jnp.float32)
                work[level, part, start:end, :] = (forward - value).astype(jnp.bfloat16)
        for start, end, value in upper_rows(inv_t.at[level], work.at[level, part]):
            solved[level, part, start:end, :] = value.astype(jnp.bfloat16)
        if level > 0:
            down_copy(level - 1, part).start()
        out_copy(level, part).start()

    def picked(level, part, member):
        wanted = jnp.full((BLK, part_cols), member, jnp.int32)
        value = solved[level, part, :BLK, :].astype(jnp.float32)
        for block in range(1, rows // BLK):
            other = solved[level, part, block * BLK : (block + 1) * BLK, :]
            value = jnp.where(wanted == block, other.astype(jnp.float32), value)
        return value

    def add_energy(level, part):
        start = pl.multiple_of(part * part_cols, part_cols)
        spectral = weights[:, pl.ds(start, part_cols)]
        for group in range(groups):
            first_member = levels - 1 + 2 * (level * groups + group)
            halves = [picked(level, part, packed[first_member + half]) for half in (0, 1)]
            stacked = jnp.concatenate(halves, axis=0)
            pushed = jnp.dot(
                stiff[level, group],
                stacked.astype(jnp.bfloat16),
                preferred_element_type=jnp.float32,
            )
            product = stacked * pushed
            folded = jnp.sum(product.reshape(-1, 8, part_cols), axis=0)
            energy[level * groups + group] += folded * spectral

    def turn(source, target):
        for start in range(0, rows, BLK):
            target[:, start : start + BLK] = source[start : start + BLK, :].T

    inv_copy(0).wait()
    off_copy(0).wait()

    def first(step, carry):
        @pl.when(step < parts)
        def _():
            go_up(0, step)

        @pl.when(step == 0)
        def _():
            inv_copy(1).wait()
            off_copy(1).wait()

        @pl.when(step > 0)
        def _():
            go_up(1, step - 1)

        return carry

    lax.fori_loop(0, parts + 1, first, 0)

    for level in range(2, levels):
        inv_copy(level).wait()
        if level + 1 < levels:
            off_copy(level).wait()
    for level in reversed(range(levels)):
        turn(inv.at[level], inv_t.at[level])
        if level + 1 < levels:
            turn(off.at[level], off_t.at[level])
    for level in range(levels):
        stiff_copy(level).wait()

    def second(step, carry):
        @pl.when(step >= 2)
        def _():
            go_down(2, step - 2)

        @pl.when((step >= 1) & (step < parts + 1))
        def _():
            go_up(3, step - 1)
            go_down(3, step - 1)

        @pl.when((step >= 2) & (step < parts))
        def _():
            add_energy(3, step - 2)
            add_energy(2, step - 2)

        @pl.when(step < parts)
        def _():
            go_up(2, step)

        return carry

    lax.fori_loop(0, parts + 2, second, 0)

    def third(step, carry):
        @pl.when(step >= max(parts - 2, 0))
        def _():
            add_energy(3, step)
            add_energy(2, step)

        go_down(1, step)
        add_energy(1, step)
        go_down(0, step)
        add_energy(0, step)
        return carry

    lax.fori_loop(0, parts, third, 0)

    by_lane = jnp.sum(energy[...], axis=1)
    folded = by_lane[:, :128]
    for start in range(128, part_cols, 128):
        folded = folded + by_lane[:, start : start + 128]
    energy_sum[...] = folded
    for step in range(1, load_count):
        energy_copy(step).start()
    total = folded
    for step in range(1, load_count):
        energy_copy(step).wait_recv()
        total = total + energy_land[step - 1]
    totals = jnp.sum(total, axis=1, keepdims=True) * (
        1.0 / (load_count * parts * part_cols * stiff.shape[2])
    )
    shape = (levels * groups, 128)
    lane = lax.broadcasted_iota(jnp.int32, shape, 1)
    row = lax.broadcasted_iota(jnp.int32, shape, 0)
    spread = jnp.where(lane == row % groups, jnp.broadcast_to(totals, shape), 0.0)
    for level in range(levels):
        energy_out[level : level + 1, :] = jnp.sum(
            spread[level * groups : (level + 1) * groups], axis=0, keepdims=True
        )[:, :groups]

    def finish(part, carry):
        for level in range(levels):
            out_copy(level, part).wait()
        for level in range(levels - 1):
            up_copy(level, part).wait_send()
            down_copy(level, part).wait_send()
        return carry

    lax.fori_loop(0, parts, finish, 0)
    for step in range(1, load_count):
        energy_copy(step).wait_send()


def on_device(col_count, load_count, *args):
    load_cols, weights, inv_diag, off_diag, crosses, members, stiffness = args
    levels, _, rows, local_cols = load_cols.shape
    groups, pair_rows = stiffness.shape[2:4]
    part_cols = PART if local_cols % PART == 0 else local_cols
    parts = local_cols // part_cols
    dense = jnp.bfloat16
    buffer = (parts, rows, part_cols)
    dma = pltpu.SemaphoreType.DMA
    anywhere = pl.BlockSpec(memory_space=pl.ANY)
    in_vmem = pl.BlockSpec(memory_space=pltpu.VMEM)
    in_smem = pl.BlockSpec(memory_space=pltpu.SMEM)
    solved, energy = pl.pallas_call(
        functools.partial(kernel, col_count, load_count),
        out_shape=(
            jax.ShapeDtypeStruct(load_cols.shape, dense),
            jax.ShapeDtypeStruct((levels, groups), jnp.float32),
        ),
        in_specs=[anywhere, in_vmem, anywhere, anywhere, in_smem, anywhere],
        out_specs=(anywhere, in_vmem),
        scratch_shapes=[
            pltpu.VMEM((levels,) + buffer, dense),
            pltpu.VMEM((levels,) + buffer, dense),
            pltpu.VMEM((levels - 1,) + buffer, dense),
            pltpu.VMEM((levels - 1,) + buffer, dense),
            pltpu.VMEM((levels - 1,) + buffer, dense),
            pltpu.VMEM((levels - 1,) + buffer, dense),
            pltpu.VMEM((rows, part_cols), dense),
            pltpu.VMEM((levels, rows, rows), dense),
            pltpu.VMEM((levels - 1, rows, rows), dense),
            pltpu.VMEM((levels, rows, rows), dense),
            pltpu.VMEM((levels - 1, rows, rows), dense),
            pltpu.VMEM((levels, groups, pair_rows, pair_rows), dense),
            pltpu.VMEM((levels * groups, 8, part_cols), jnp.float32),
            pltpu.VMEM((levels * groups, 128), jnp.float32),
            pltpu.VMEM((load_count - 1, levels * groups, 128), jnp.float32),
            dma((levels, parts)),
            dma((levels,)),
            dma((levels - 1,)),
            dma((levels,)),
            dma((levels, parts)),
            dma((levels - 1, parts)),
            dma((levels - 1, parts)),
            dma((levels - 1, parts)),
            dma((levels - 1, parts)),
            dma((load_count - 1,)),
            dma((load_count - 1,)),
        ],
        compiler_params=pltpu.CompilerParams(
            collective_id=0, has_side_effects=True, vmem_limit_bytes=56 * 2**20
        ),
    )(
        load_cols,
        weights.reshape(1, local_cols),
        inv_diag,
        off_diag,
        jnp.concatenate([crosses.reshape(-1), members.reshape(-1)]),
        stiffness,
    )
    return solved, energy.reshape(levels, 1, groups)


def solution(mesh):
    placed = (
        P(None, "col", None, ("groups", "load")),
        P(("groups", "load")),
        P(None, "col", None, None),
        P(None, "col", None, None),
        P(None, "col"),
        P(None, "col", None, None),
        P(None, "col", None, None, None),
    )
    return jax.shard_map(
        functools.partial(on_device, mesh.shape["col"], mesh.shape["load"]),
        mesh=mesh,
        in_specs=placed,
        out_specs=(P(None, "col", None, ("groups", "load")), P("groups", "col", None)),
        check_vma=False,
    )
```

```python
import functools

import jax
import jax.numpy as jnp
from jax import lax
from jax.experimental import pallas as pl
from jax.experimental.pallas import tpu as pltpu
from jax.sharding import PartitionSpec as P

MESH = pl.DeviceIdType.MESH
TILE = 256
PART = 256
BLK = 128


def row_tiles(size):
    return [(start, min(start + TILE, size)) for start in range(0, size, TILE)]


def lower_rows(matrix, columns):
    for start, end in row_tiles(matrix.shape[0]):
        yield start, end, jnp.dot(
            matrix[start:end, :end], columns[:end, :], preferred_element_type=jnp.float32
        )


def upper_rows(matrix, columns):
    for start, end in row_tiles(matrix.shape[0]):
        yield start, end, jnp.dot(
            matrix[start:end, start:], columns[start:, :], preferred_element_type=jnp.float32
        )


def full_rows(matrix, columns):
    for start, end in row_tiles(matrix.shape[0]):
        yield start, end, jnp.dot(
            matrix[start:end, :], columns[...], preferred_element_type=jnp.float32
        )


def kernel(
    col_count,
    load_count,
    load_hbm,
    weights,
    inv_hbm,
    off_hbm,
    packed,
    stiff_hbm,
    out_hbm,
    energy_out,
    work,
    solved,
    kept,
    outgoing,
    up_land,
    down_land,
    rhs,
    inv,
    off,
    inv_t,
    off_t,
    stiff,
    energy,
    energy_sum,
    energy_land,
    load_sem,
    inv_sem,
    off_sem,
    stiff_sem,
    out_sem,
    up_send,
    up_recv,
    down_send,
    down_recv,
    energy_send,
    energy_recv,
):
    levels, parts, rows, part_cols = work.shape
    groups = stiff.shape[1]
    bit_count = col_count.bit_length() - 1
    my_col = lax.axis_index("col")
    my_load = lax.axis_index("load")

    def partner(level):
        mask = 1 << (level % bit_count)
        return my_col + mask - 2 * mask * (my_col // mask % 2)

    def load_peer(step):
        return lax.rem(my_load + step, load_count)

    def load_copy(level, part):
        start = part * part_cols
        return pltpu.make_async_copy(
            load_hbm.at[level, 0, :, pl.ds(pl.multiple_of(start, part_cols), part_cols)],
            work.at[level, part],
            load_sem.at[level, part],
        )

    def inv_copy(level):
        return pltpu.make_async_copy(inv_hbm.at[level, 0], inv.at[level], inv_sem.at[level])

    def off_copy(level):
        return pltpu.make_async_copy(off_hbm.at[level, 0], off.at[level], off_sem.at[level])

    def stiff_copy(level):
        return pltpu.make_async_copy(stiff_hbm.at[level, 0], stiff.at[level], stiff_sem.at[level])

    def out_copy(level, part):
        start = part * part_cols
        return pltpu.make_async_copy(
            solved.at[level, part],
            out_hbm.at[level, 0, :, pl.ds(pl.multiple_of(start, part_cols), part_cols)],
            out_sem.at[level, part],
        )

    def up_copy(level, part):
        return pltpu.make_async_remote_copy(
            src_ref=outgoing.at[level, part],
            dst_ref=up_land.at[level, part],
            send_sem=up_send.at[level, part],
            recv_sem=up_recv.at[level, part],
            device_id={"col": partner(level)},
            device_id_type=MESH,
        )

    def down_copy(level, part):
        return pltpu.make_async_remote_copy(
            src_ref=solved.at[level + 1, part],
            dst_ref=down_land.at[level, part],
            send_sem=down_send.at[level, part],
            recv_sem=down_recv.at[level, part],
            device_id={"col": partner(level)},
            device_id_type=MESH,
        )

    def energy_copy(step):
        return pltpu.make_async_remote_copy(
            src_ref=energy_sum,
            dst_ref=energy_land.at[step - 1],
            send_sem=energy_send.at[step - 1],
            recv_sem=energy_recv.at[step - 1],
            device_id={"load": load_peer(step)},
            device_id_type=MESH,
        )

    barrier = pltpu.get_barrier_semaphore()
    used_bits = sorted({level % bit_count for level in range(levels - 1)})
    for bit in used_bits:
        pl.semaphore_signal(
            barrier, inc=1, device_id={"col": partner(bit)}, device_id_type=MESH
        )
    for step in range(1, load_count):
        pl.semaphore_signal(
            barrier, inc=1, device_id={"load": load_peer(step)}, device_id_type=MESH
        )

    inv_copy(0).start()
    load_copy(0, 0).start()
    off_copy(0).start()
    inv_copy(1).start()
    load_copy(0, 1).start()
    load_copy(1, 0).start()
    off_copy(1).start()
    load_copy(1, 1).start()
    for part in range(2, parts):
        load_copy(0, part).start()
        load_copy(1, part).start()
    for level in range(2, levels):
        inv_copy(level).start()
        if level + 1 < levels:
            off_copy(level).start()
        for part in range(parts):
            load_copy(level, part).start()
    for level in reversed(range(levels)):
        stiff_copy(level).start()

    energy[...] = jnp.zeros_like(energy)

    def greeted():
        pl.semaphore_wait(barrier, len(used_bits) + load_count - 1)

    def crosses_here(level, shape):
        return jnp.full(shape, packed[level], jnp.int32) == 1

    def go_up(level, part, opening=False):
        load_copy(level, part).wait()
        if level == 0:
            right_side = work.at[level, part]
        else:
            up_copy(level - 1, part).wait_recv()
            incoming = kept[level - 1, part].astype(jnp.float32) + up_land[
                level - 1, part
            ].astype(jnp.float32)
            rhs[...] = (work[level, part].astype(jnp.float32) - incoming).astype(jnp.bfloat16)
            right_side = rhs
        results = [
            (start, end, value.astype(jnp.bfloat16))
            for start, end, value in lower_rows(inv.at[level], right_side)
        ]
        for start, end, value in results:
            work[level, part, start:end, :] = value
        if level + 1 < levels:
            for start, end, value in full_rows(off.at[level], work.at[level, part]):
                crossing = crosses_here(level, value.shape)
                outgoing[level, part, start:end, :] = jnp.where(crossing, value, 0.0).astype(
                    jnp.bfloat16
                )
                kept[level, part, start:end, :] = jnp.where(crossing, 0.0, value).astype(
                    jnp.bfloat16
                )
            if opening:
                greeted()
            up_copy(level, part).start()

    def go_down(level, part):
        if level + 1 < levels:
            down_copy(level, part).wait_recv()
            rhs[...] = jnp.where(
                crosses_here(level, rhs.shape),
                down_land[level, part].astype(jnp.float32),
                solved[level + 1, part].astype(jnp.float32),
            ).astype(jnp.bfloat16)
            for start, end, value in full_rows(off_t.at[level], rhs):
                forward = work[level, part, start:end, :].astype(jnp.float32)
                work[level, part, start:end, :] = (forward - value).astype(jnp.bfloat16)
        for start, end, value in upper_rows(inv_t.at[level], work.at[level, part]):
            solved[level, part, start:end, :] = value.astype(jnp.bfloat16)
        if level > 0:
            down_copy(level - 1, part).start()
        out_copy(level, part).start()

    def picked(level, part, member):
        wanted = jnp.full((BLK, part_cols), member, jnp.int32)
        value = solved[level, part, :BLK, :].astype(jnp.float32)
        for block in range(1, rows // BLK):
            other = solved[level, part, block * BLK : (block + 1) * BLK, :]
            value = jnp.where(wanted == block, other.astype(jnp.float32), value)
        return value

    def add_energy(level, part):
        start = pl.multiple_of(part * part_cols, part_cols)
        spectral = weights[:, pl.ds(start, part_cols)]
        for group in range(groups):
            first_member = levels - 1 + 2 * (level * groups + group)
            halves = [picked(level, part, packed[first_member + half]) for half in (0, 1)]
            stacked = jnp.concatenate(halves, axis=0)
            pushed = jnp.dot(
                stiff[level, group],
                stacked.astype(jnp.bfloat16),
                preferred_element_type=jnp.float32,
            )
            product = stacked * pushed
            folded = jnp.sum(product.reshape(-1, 8, part_cols), axis=0)
            energy[level * groups + group] += folded * spectral

    def turn(source, target):
        for start in range(0, rows, BLK):
            target[:, start : start + BLK] = source[start : start + BLK, :].T

    inv_copy(0).wait()
    off_copy(0).wait()

    go_up(0, 0, opening=True)
    inv_copy(1).wait()
    off_copy(1).wait()

    def first(step, carry):
        go_up(1, step - 1)

        @pl.when(step < parts)
        def _():
            go_up(0, step)

        return carry

    lax.fori_loop(1, parts + 1, first, 0)

    for level in range(2, levels):
        inv_copy(level).wait()
        if level + 1 < levels:
            off_copy(level).wait()
    for level in reversed(range(levels)):
        turn(inv.at[level], inv_t.at[level])
        if level + 1 < levels:
            turn(off.at[level], off_t.at[level])
    for level in range(levels):
        stiff_copy(level).wait()

    def second(step, carry):
        @pl.when(step >= 2)
        def _():
            go_down(2, step - 2)

        @pl.when((step >= 1) & (step < parts + 1))
        def _():
            go_up(3, step - 1)
            go_down(3, step - 1)

        @pl.when((step >= 2) & (step < parts))
        def _():
            add_energy(3, step - 2)
            add_energy(2, step - 2)

        @pl.when(step < parts)
        def _():
            go_up(2, step)

        return carry

    lax.fori_loop(0, parts + 2, second, 0)

    def third(step, carry):
        @pl.when(step >= max(parts - 2, 0))
        def _():
            add_energy(3, step)
            add_energy(2, step)

        go_down(1, step)
        add_energy(1, step)
        go_down(0, step)
        add_energy(0, step)
        return carry

    lax.fori_loop(0, parts, third, 0)

    by_lane = jnp.sum(energy[...], axis=1)
    folded = by_lane[:, :128]
    for start in range(128, part_cols, 128):
        folded = folded + by_lane[:, start : start + 128]
    energy_sum[...] = folded
    for step in range(1, load_count):
        energy_copy(step).start()
    total = folded
    for step in range(1, load_count):
        energy_copy(step).wait_recv()
        total = total + energy_land[step - 1]
    totals = jnp.sum(total, axis=1, keepdims=True) * (
        1.0 / (load_count * parts * part_cols * stiff.shape[2])
    )
    shape = (levels * groups, 128)
    lane = lax.broadcasted_iota(jnp.int32, shape, 1)
    row = lax.broadcasted_iota(jnp.int32, shape, 0)
    spread = jnp.where(lane == row % groups, jnp.broadcast_to(totals, shape), 0.0)
    for level in range(levels):
        energy_out[level : level + 1, :] = jnp.sum(
            spread[level * groups : (level + 1) * groups], axis=0, keepdims=True
        )[:, :groups]

    def finish(part, carry):
        for level in range(levels):
            out_copy(level, part).wait()
        for level in range(levels - 1):
            up_copy(level, part).wait_send()
            down_copy(level, part).wait_send()
        return carry

    lax.fori_loop(0, parts, finish, 0)
    for step in range(1, load_count):
        energy_copy(step).wait_send()


def on_device(col_count, load_count, *args):
    load_cols, weights, inv_diag, off_diag, crosses, members, stiffness = args
    levels, _, rows, local_cols = load_cols.shape
    groups, pair_rows = stiffness.shape[2:4]
    part_cols = PART if local_cols % PART == 0 else local_cols
    parts = local_cols // part_cols
    dense = jnp.bfloat16
    buffer = (parts, rows, part_cols)
    dma = pltpu.SemaphoreType.DMA
    anywhere = pl.BlockSpec(memory_space=pl.ANY)
    in_vmem = pl.BlockSpec(memory_space=pltpu.VMEM)
    in_smem = pl.BlockSpec(memory_space=pltpu.SMEM)
    solved, energy = pl.pallas_call(
        functools.partial(kernel, col_count, load_count),
        out_shape=(
            jax.ShapeDtypeStruct(load_cols.shape, dense),
            jax.ShapeDtypeStruct((levels, groups), jnp.float32),
        ),
        in_specs=[anywhere, in_vmem, anywhere, anywhere, in_smem, anywhere],
        out_specs=(anywhere, in_vmem),
        scratch_shapes=[
            pltpu.VMEM((levels,) + buffer, dense),
            pltpu.VMEM((levels,) + buffer, dense),
            pltpu.VMEM((levels - 1,) + buffer, dense),
            pltpu.VMEM((levels - 1,) + buffer, dense),
            pltpu.VMEM((levels - 1,) + buffer, dense),
            pltpu.VMEM((levels - 1,) + buffer, dense),
            pltpu.VMEM((rows, part_cols), dense),
            pltpu.VMEM((levels, rows, rows), dense),
            pltpu.VMEM((levels - 1, rows, rows), dense),
            pltpu.VMEM((levels, rows, rows), dense),
            pltpu.VMEM((levels - 1, rows, rows), dense),
            pltpu.VMEM((levels, groups, pair_rows, pair_rows), dense),
            pltpu.VMEM((levels * groups, 8, part_cols), jnp.float32),
            pltpu.VMEM((levels * groups, 128), jnp.float32),
            pltpu.VMEM((load_count - 1, levels * groups, 128), jnp.float32),
            dma((levels, parts)),
            dma((levels,)),
            dma((levels - 1,)),
            dma((levels,)),
            dma((levels, parts)),
            dma((levels - 1, parts)),
            dma((levels - 1, parts)),
            dma((levels - 1, parts)),
            dma((levels - 1, parts)),
            dma((load_count - 1,)),
            dma((load_count - 1,)),
        ],
        compiler_params=pltpu.CompilerParams(
            collective_id=0, has_side_effects=True, vmem_limit_bytes=56 * 2**20
        ),
    )(
        load_cols,
        weights.reshape(1, local_cols),
        inv_diag,
        off_diag,
        jnp.concatenate([crosses.reshape(-1), members.reshape(-1)]),
        stiffness,
    )
    return solved, energy.reshape(levels, 1, groups)


def solution(mesh):
    placed = (
        P(None, "col", None, ("groups", "load")),
        P(("groups", "load")),
        P(None, "col", None, None),
        P(None, "col", None, None),
        P(None, "col"),
        P(None, "col", None, None),
        P(None, "col", None, None, None),
    )
    return jax.shard_map(
        functools.partial(on_device, mesh.shape["col"], mesh.shape["load"]),
        mesh=mesh,
        in_specs=placed,
        out_specs=(P(None, "col", None, ("groups", "load")), P("groups", "col", None)),
        check_vma=False,
    )
```
